32 devices in a mesh: pipe: 2 (over x), expert: 16 (over z, y, core).
Axes of the slice: x: 2, y: 2, z: 4, core: 2. Of those that a mesh axis runs over, the one named last changes fastest.
Arguments:
- out_grad: bfloat16 [2, 2048, 2560], P('pipe', 'expert'), may hold values from -1.5 to 1.5
- layer_input: bfloat16 [2, 2048, 2560], P('pipe', 'expert'), may hold values from -6 to 6
- route_ids: int32 [2, 2048, 6], P('pipe', 'expert'), may hold values from 0 to 15, all different within a row; in each aligned block of 128 rows (0 to 127, 128 to 255, ..., all dimensions but the last counted through in order) at most 56 rows name the same one
- route_probs: float32 [2, 2048, 6], P('pipe', 'expert'), may hold values from 0.03 to 0.5
- gate_weight: bfloat16 [2, 16, 2560, 768], P('pipe', 'expert'), may hold values from -0.125 to 0.125
- up_weight: bfloat16 [2, 16, 2560, 768], P('pipe', 'expert'), may hold values from -0.125 to 0.125
- down_weight: bfloat16 [2, 16, 768, 2560], P('pipe', 'expert'), may hold values from -0.21875 to 0.21875
Outputs:
- prev_grad: bfloat16 [2, 2048, 2560], P('pipe', 'expert')
- gate_grad: bfloat16 [2, 2048, 6], P('pipe', 'expert')
The draws below stay inside these ranges and needn't reach their ends.
Inputs may be any that keep to these rules, and one draw needn't show every extreme that they name: `route_ids`: each token names 6 different experts; the 128 tokens of one aligned block name one expert at most 56 times, and some block reaches 56.
All inputs are finite; a program needn't handle non-finite values.
Results may differ from the reference program's by a relative error of at most 0.004.
Values may be sent and summed in bfloat16 or wider, within the bound.
A program may use at most 128 MiB of HBM per device.

```python
import math
import jax
import jax.numpy as jnp
import numpy as np
from jax import lax

D = 2560
F = 768
TOPK = 6
TOK_DEV = 128
SECTIONS = 2
EXPERTS = 16
TOKENS = 2048
CAP = 56
N_EXPERT = 16


def steps_of(rng, extent, shards, smallest, largest):
    factor_of = 1.0
    for axis_at, parts in shards:
        heights = jax.random.uniform(jax.random.fold_in(jax.random.fold_in(rng, 6), axis_at), (parts,), jnp.float32, smallest / len(shards), largest / len(shards))
        factor_of = factor_of * jnp.repeat(jnp.exp(heights), extent[axis_at] // parts).reshape((-1,) + (1,) * (len(extent) - 1 - axis_at))
    return factor_of


def assign_block(own_key, own, number, rows, count, top, bound, skew):
    ranking = jax.random.permutation(own_key, count)
    packed, ordinary = shares(count, rows * top, bound, skew, True), shares(count, rows * top, bound, skew, False)
    places = jnp.arange(count)

    def named(sizes, offset_by):
        used = int((sizes > 0).sum())
        fixed = max(1, used // 4)
        shifted = fixed + (places - fixed + offset_by * (used - fixed)) % max(1, count - fixed)
        return jnp.zeros((count,), jnp.int32).at[ranking[jnp.where(places < fixed, places, shifted)]].set(jnp.asarray(sizes, jnp.int32))

    sizes = jnp.where(number % 4 == 0, named(packed, number // 4), named(ordinary, number - number // 4 - 1))
    mixed = jax.random.permutation(jax.random.fold_in(own, 3), count)
    source_of, receiver = mixed[0:count // 2 * 2:2], mixed[1:count // 2 * 2:2]
    room = jnp.minimum(sizes[source_of] - 1, bound - sizes[receiver]) // 2
    room = jnp.where((source_of == ranking[0]) | (receiver == ranking[0]) | (sizes[receiver] == 0), 0, jnp.maximum(room, 0))
    shifted = jax.random.randint(jax.random.fold_in(own, 4), (count // 2,), 0, 1 << 20) % (room + 1)
    sizes = sizes.at[source_of].add(-shifted).at[receiver].add(shifted)
    members = jnp.searchsorted(jnp.cumsum(sizes), jnp.arange(rows * top), side="right").astype(jnp.int32)
    table = members.reshape(top, rows).T
    table = table[jax.random.permutation(jax.random.fold_in(own, 1), rows)]
    offset_by = jax.random.randint(jax.random.fold_in(own, 2), (rows, 1), 0, top)
    return jnp.take_along_axis(table, (jnp.arange(top)[None, :] + offset_by) % top, axis=1)


def shares(number_of, total, reach, lean, full):
    portions = [(1 << 20) // math.isqrt(standing ** lean) + 1 for standing in range(1, number_of + 1)]
    largest = reach if full else min(reach, max(-(-total // number_of), total * portions[0] // sum(portions)))
    least = 1 if total - largest >= number_of - 1 else 0
    counts, rest = [largest] + [least] * (number_of - 1), total - largest - least * (number_of - 1)
    while rest > 0:
        movable = [i for i in range(1, number_of) if counts[i] < largest] or [i for i in range(1, number_of) if counts[i] < reach]
        whole, left = sum([portions[i] for i in movable]), rest
        for i in movable:
            addition = min(reach - counts[i], max(1, left * portions[i] // whole), rest)
            counts[i] = counts[i] + addition
            rest = rest - addition
    return np.array(counts)


def centred(rng, extent, scale, bound, split=(), kind=jnp.bfloat16):
    array = jax.random.normal(rng, extent, jnp.float32) * scale
    if len(split) > 0:
        array = steps_of(rng, extent, split, -0.22, 0.18) * array
    return jnp.clip(array, min=-bound, max=bound).astype(kind)


def setup_inputs(seed: int = 0) -> dict:
    splits = jax.random.split(jax.random.key(seed), 8)
    out_grad = centred(splits[0], (SECTIONS, TOKENS, D), 0.25, 1.5, ((0, 2), (1, 16)))
    layer_input = centred(splits[1], (SECTIONS, TOKENS, D), 1.0, 6.0, ((0, 2), (1, 16)))
    route_ids_keys = jax.random.split(jax.random.fold_in(splits[2], 1), SECTIONS * TOKENS // TOK_DEV)
    route_ids_turns = jax.random.permutation(jax.random.fold_in(splits[2], 3), SECTIONS * TOKENS // TOK_DEV)
    route_ids = jax.vmap(lambda own, number: assign_block(jax.random.fold_in(splits[2], 2), own, number, TOK_DEV, EXPERTS, TOPK, CAP, 1))(route_ids_keys, route_ids_turns).reshape((SECTIONS, TOKENS, TOPK))
    route_probs = jnp.clip(jnp.exp(math.log(0.5) - 2.8134107 * jax.random.uniform(splits[3], (SECTIONS, TOKENS, TOPK), jnp.float32) ** steps_of(splits[3], (SECTIONS, TOKENS, TOPK), ((0, 2), (1, 16)), -0.2, 0.2)), 0.03, 0.5)
    gate_weight = centred(splits[4], (SECTIONS, EXPERTS, D, F), D ** -0.5, 0.125, ((0, 2), (1, 16)))
    up_weight = centred(splits[5], (SECTIONS, EXPERTS, D, F), D ** -0.5, 0.125, ((0, 2), (1, 16)))
    down_weight = centred(splits[6], (SECTIONS, EXPERTS, F, D), F ** -0.5, 0.21875, ((0, 2), (1, 16)))
    return {"out_grad": out_grad, "layer_input": layer_input, "route_ids": route_ids, "route_probs": route_probs, "gate_weight": gate_weight, "up_weight": up_weight, "down_weight": down_weight}


def expert_rows(grad_rows, input_rows, gate_matrix, up_matrix, down_matrix):
    gate_pre = jnp.dot(input_rows, gate_matrix, preferred_element_type=jnp.float32)
    up_pre = jnp.dot(input_rows, up_matrix, preferred_element_type=jnp.float32)
    hidden_grad = jnp.dot(grad_rows, down_matrix.T, preferred_element_type=jnp.float32)
    sigmoid = jax.nn.sigmoid(gate_pre)
    active = gate_pre * sigmoid
    gate_value = jnp.sum(hidden_grad * active * up_pre, axis=-1).astype(jnp.bfloat16)
    gate_back = (hidden_grad * up_pre * sigmoid * (1.0 + gate_pre * (1.0 - sigmoid))).astype(jnp.bfloat16)
    up_back = (hidden_grad * active).astype(jnp.bfloat16)
    input_back = jnp.dot(gate_back, gate_matrix.T, preferred_element_type=jnp.float32) + jnp.dot(up_back, up_matrix.T, preferred_element_type=jnp.float32)
    return input_back.astype(jnp.bfloat16), gate_value


def section_pass(section_args):
    grad_tokens, input_tokens, chosen, slot_probs, gate_all, up_all, down_all = section_args
    block_ids = chosen.reshape(N_EXPERT, TOK_DEV * TOPK)
    one_hot = (block_ids[:, :, None] == jnp.arange(EXPERTS, dtype=jnp.int32)[None, None, :]).astype(jnp.int32)
    places = jnp.sum(one_hot * jnp.cumsum(one_hot, axis=1), axis=2) - 1
    target = (block_ids * CAP + places).astype(jnp.int32)
    block_rows = jnp.arange(N_EXPERT, dtype=jnp.int32)[:, None]
    values = jnp.broadcast_to(jnp.arange(TOK_DEV * TOPK, dtype=jnp.int32)[None, :], target.shape)
    slot_table = jnp.full((N_EXPERT, EXPERTS * CAP), -1, jnp.int32).at[block_rows, target].set(values)
    slot_table = slot_table.reshape(N_EXPERT, EXPERTS, CAP).transpose(1, 0, 2).reshape(EXPERTS, N_EXPERT * CAP)
    block_index = jnp.repeat(jnp.arange(N_EXPERT, dtype=jnp.int32), CAP)

    def per_expert(carry, inputs):
        running, gate_sum = carry
        slots, gate_matrix, up_matrix, down_matrix = inputs
        filled = slots >= 0
        local_slot = jnp.where(filled, slots, 0)
        token_index = (block_index * TOK_DEV + local_slot // TOPK).astype(jnp.int32)
        slot_index = (local_slot % TOPK).astype(jnp.int32)
        zero_value = jnp.zeros((), grad_tokens.dtype)
        grad_rows = jnp.where(filled[:, None], grad_tokens[token_index], zero_value)
        input_rows = jnp.where(filled[:, None], input_tokens[token_index], zero_value)
        input_back, gate_value = expert_rows(grad_rows, input_rows, gate_matrix, up_matrix, down_matrix)
        weight = jnp.where(filled, slot_probs[token_index, slot_index], jnp.zeros((), slot_probs.dtype))
        running = running.at[token_index].add(weight[:, None] * input_back.astype(slot_probs.dtype))
        gate_sum = gate_sum.at[token_index, slot_index].add(jnp.where(filled, gate_value.astype(slot_probs.dtype), jnp.zeros((), slot_probs.dtype)))
        return (running, gate_sum), None

    start = (grad_tokens.astype(jnp.float32), jnp.zeros((TOKENS, TOPK), jnp.float32))
    (running, gate_sum), unused = lax.scan(per_expert, start, (slot_table, gate_all, up_all, down_all))
    return running.astype(jnp.bfloat16), gate_sum.astype(jnp.bfloat16)


def reference(out_grad, layer_input, route_ids, route_probs, gate_weight, up_weight, down_weight):
    input_grad, gate_grad = lax.map(section_pass, (out_grad, layer_input, route_ids, route_probs, gate_weight, up_weight, down_weight))
    prev_grad = jnp.concatenate([input_grad[1:], jnp.zeros_like(input_grad[:1])], axis=0)
    return prev_grad, gate_grad
```

```python
import jax
import jax.numpy as jnp
from jax import lax
from jax.sharding import PartitionSpec as P

F32, BF16 = jnp.float32, jnp.bfloat16


def body(out_grad, layer_input, route_ids, route_probs, gate_weight, up_weight, down_weight):
    grad, inputs, ids, probs = out_grad[0], layer_input[0], route_ids[0], route_probs[0]
    gate_w, up_w, down_w = gate_weight[0, 0], up_weight[0, 0], down_weight[0, 0]
    peers = lax.axis_size("expert")
    tokens, top = ids.shape
    cap = min(tokens, 7 * tokens * top // (6 * peers))
    chosen = ids[:, :, None] == jnp.arange(peers, dtype=jnp.int32)
    weights = jnp.sum(jnp.where(chosen, probs[:, :, None], 0.0), axis=1).T
    mine = lax.all_to_all(weights, "expert", 0, 0, tiled=True)
    grad_all = lax.all_gather(grad, "expert")
    input_all = lax.all_gather(inputs, "expert")
    used = mine > 0
    place = jnp.cumsum(used.astype(jnp.int32), axis=1) - 1
    pick = (place[:, None, :] == jnp.arange(cap)[None, :, None]) & used[:, None, :]
    pick16 = pick.astype(BF16)
    grad_rows = jnp.einsum("bst,btd->bsd", pick16, grad_all).reshape(peers * cap, -1)
    input_rows = jnp.einsum("bst,btd->bsd", pick16, input_all).reshape(peers * cap, -1)
    gate_pre = jnp.dot(input_rows, gate_w, preferred_element_type=F32)
    up_pre = jnp.dot(input_rows, up_w, preferred_element_type=F32)
    hidden = lax.dot_general(grad_rows, down_w, (((1,), (1,)), ((), ())), preferred_element_type=F32)
    sig = jax.nn.sigmoid(gate_pre)
    active = gate_pre * sig
    gate_value = jnp.sum(hidden * active * up_pre, axis=-1).reshape(peers, cap)
    gate_part = (hidden * up_pre * sig * (1.0 + gate_pre * (1.0 - sig))).astype(BF16)
    up_part = (hidden * active).astype(BF16)
    back = jnp.dot(gate_part, gate_w.T, preferred_element_type=F32) + jnp.dot(
        up_part, up_w.T, preferred_element_type=F32
    )
    slot_weight = jnp.sum(jnp.where(pick, mine[:, None, :], 0.0), axis=2)
    back = (back.astype(BF16).astype(F32) * slot_weight.reshape(-1, 1)).astype(BF16)
    part = jnp.einsum("bst,bsd->btd", pick16, back.reshape(peers, cap, -1))
    total = lax.psum_scatter(part, "expert", scatter_dimension=0, tiled=False)
    combined = grad.astype(F32) + total.astype(F32)
    gates = jnp.sum(jnp.where(pick, gate_value[:, :, None], 0.0), axis=1)
    gates = lax.all_to_all(gates, "expert", 0, 0, tiled=True)
    gate_slot = jnp.sum(jnp.where(chosen, gates.T[:, None, :], 0.0), axis=2).astype(BF16)
    count = lax.axis_size("pipe")
    passed = lax.ppermute(combined.astype(BF16), "pipe", [(s, s - 1) for s in range(1, count)])
    return passed[None], gate_slot[None]


def solution(mesh):
    rows = P("pipe", "expert", None)
    mats = P("pipe", "expert", None, None)
    return jax.shard_map(
        body,
        mesh=mesh,
        in_specs=(rows,) * 4 + (mats,) * 3,
        out_specs=(rows, rows),
        check_vma=False,
    )
```

```python
import functools

import jax
import jax.numpy as jnp
from jax import lax
from jax.experimental import pallas as pl
from jax.experimental.pallas import tpu as pltpu
from jax.sharding import PartitionSpec as P

F32, BF16 = jnp.float32, jnp.bfloat16
MESH = pl.DeviceIdType.MESH
NT = (((1,), (1,)), ((), ()))


def dot(a, b, dims=(((1,), (0,)), ((), ()))):
    return lax.dot_general(a, b, dims, preferred_element_type=F32)


def kernel(
    nz, ny, slots, pipes,
    grad_ref, input_ref, send_w_ref, gate_hbm, up_hbm, down_hbm,
    out_ref, gates_ref, all_ref,
    gate_w, up_w, down_w, blocks, rows, parts, hidden, scaled, slot_w, route, gate_send,
    core_recv, y_send, y_recv, z_send, z_recv, total, final, zeros,
    load_sem, own_sem, block_sem, zero_sem, ag_send, ag_recv, w_send, w_recv, g_send, g_recv,
    c_send_sem, c_recv_sem, y_send_sem, y_recv_sem, z_send_sem, z_recv_sem, p_sem,
):
    peers = nz * ny * 2
    count = 2 * ny
    tokens, width = grad_ref.shape
    inner = gate_w.shape[1]
    stage = lax.axis_index("pipe")
    me = lax.axis_index("expert")
    core = lax.rem(me, 2)
    yy = lax.rem(lax.div(me, 2), ny)
    zz = lax.div(me, 2 * ny)
    sibling = me + 1 - 2 * core

    def number(z, y, c):
        return (z * ny + y) * 2 + c

    def column_of(j):
        low, high = zz, nz - 1 - zz
        near = jnp.minimum(low, high)
        half = lax.div(j + 1, 2)
        between = jnp.where(lax.rem(j, 2) == 1, zz - half, zz + half)
        far = jnp.where(low <= high, j, nz - 1 - j)
        return jnp.where(j <= 2 * near, between, far)

    def remote(src, dst, ssem, rsem, target):
        return pltpu.make_async_remote_copy(
            src_ref=src, dst_ref=dst, send_sem=ssem, recv_sem=rsem,
            device_id={"expert": target}, device_id_type=MESH,
        )

    def spread(block, kind, target):
        return remote(all_ref.at[block], all_ref.at[block], ag_send.at[block, kind], ag_recv.at[block], target)

    def arrived(block):
        spread(block, 0, sibling).wait_recv()

    def y_peer(i):
        return lax.rem(yy + i, ny)

    def plane_sends(z, act):
        block = number(z, yy, core)

        @pl.when((z <= zz) & (zz + 1 < nz))
        def _():
            act(spread(block, 1, me + 2 * ny))

        @pl.when((z >= zz) & (zz > 0))
        def _():
            act(spread(block, 2, me - 2 * ny))

        for i in range(1, ny):
            act(spread(block, 2 + i, number(zz, y_peer(i), core)))
        act(spread(block, 0, sibling))

    loads = [
        pltpu.make_async_copy(gate_hbm, gate_w, load_sem.at[0]),
        pltpu.make_async_copy(up_hbm, up_w, load_sem.at[1]),
        pltpu.make_async_copy(down_hbm, down_w, load_sem.at[2]),
    ]
    own = [
        pltpu.make_async_copy(grad_ref, all_ref.at[me, 0], own_sem.at[0]),
        pltpu.make_async_copy(input_ref, all_ref.at[me, 1], own_sem.at[1]),
    ]
    for copy in own + loads:
        copy.start()

    barrier = pltpu.get_barrier_semaphore()

    @pl.loop(1, peers)
    def _(i):
        pl.semaphore_signal(barrier, inc=1, device_id={"expert": lax.rem(me + i, peers)}, device_id_type=MESH)

    @pl.when(stage > 0)
    def _():
        pl.semaphore_signal(barrier, inc=1, device_id={"pipe": stage - 1}, device_id_type=MESH)

    @pl.when(stage < pipes - 1)
    def _():
        pl.semaphore_signal(barrier, inc=1, device_id={"pipe": stage + 1}, device_id_type=MESH)

    beside = jnp.where(stage > 0, 1, 0) + jnp.where(stage < pipes - 1, 1, 0)
    pl.semaphore_wait(barrier, peers - 1 + beside)

    def w_copy(target):
        return remote(send_w_ref.at[target], route.at[me], w_send.at[target], w_recv.at[me], target)

    def w_from(source):
        return remote(send_w_ref.at[source], route.at[source], w_send.at[source], w_recv.at[source], source)

    @pl.loop(1, peers)
    def _(i):
        w_copy(lax.rem(me + i, peers)).start()

    for copy in own:
        copy.wait()
    plane_sends(zz, lambda c: c.start())
    route[me] = send_w_ref[me]

    @pl.loop(1, peers)
    def _(i):
        w_from(lax.rem(me + i, peers)).wait_recv()

    for copy in loads:
        copy.wait()

    row_at = lax.broadcasted_iota(jnp.int32, (tokens, tokens), 0)
    col_at = lax.broadcasted_iota(jnp.int32, (tokens, tokens), 1)
    before = jnp.where(row_at < col_at, 1.0, 0.0).astype(BF16)
    slot_at = lax.broadcasted_iota(jnp.int32, (slots, tokens), 0)

    def pick_of(block):
        weight = route[block]
        used = jnp.where(weight > 0, 1.0, 0.0)
        place = dot(used.astype(BF16), before)[0:1].astype(jnp.int32)
        return (place == slot_at) & (weight[0:1] > 0), weight[0:1]

    def block_in(z, i):
        return number(z, lax.rem(i, ny), lax.div(i, ny))

    def fetch(z, i):
        return pltpu.make_async_copy(all_ref.at[block_in(z, i)], blocks.at[i], block_sem.at[i])

    def compute(z):
        @pl.loop(0, count)
        def _(i):
            fetch(z, i).start()

        @pl.loop(0, count)
        def _(i):
            fetch(z, i).wait()
            pick, weight = pick_of(block_in(z, i))
            pick16 = jnp.where(pick, 1.0, 0.0).astype(BF16)
            at = pl.ds(pl.multiple_of(i * slots, slots), slots)
            rows[0, at] = dot(pick16, blocks[i, 0]).astype(BF16)
            rows[1, at] = dot(pick16, blocks[i, 1]).astype(BF16)
            per_slot = jnp.sum(jnp.where(pick, weight, 0.0), axis=1, keepdims=True)
            slot_w[0, at] = jnp.broadcast_to(per_slot, (slots, 128))

        slot_w[1] = jnp.zeros_like(slot_w[1])
        tile = 256

        @pl.loop(0, inner // tile)
        def _(f):
            at = pl.ds(pl.multiple_of(f * tile, tile), tile)
            gate_pre = dot(rows[1], gate_w[:, at])
            up_pre = dot(rows[1], up_w[:, at])
            back = dot(rows[0], down_w[at, :], NT)
            sig = jax.nn.sigmoid(gate_pre)
            up_back = back * (gate_pre * sig)
            hidden[0, :, at] = (back * up_pre * sig * (1.0 + gate_pre * (1.0 - sig))).astype(BF16)
            hidden[1, :, at] = up_back.astype(BF16)
            value = jnp.sum(up_back * up_pre, axis=1, keepdims=True)
            slot_w[1] = slot_w[1] + jnp.broadcast_to(value, slot_w[1].shape)

        wide = 512

        @pl.loop(0, width // wide)
        def _(d):
            at = pl.ds(pl.multiple_of(d * wide, wide), wide)
            back = dot(hidden[0], gate_w[at, :], NT) + dot(hidden[1], up_w[at, :], NT)
            back = back.astype(BF16).astype(F32) * slot_w[0, :, 0:1]
            scaled[:, at] = back.astype(BF16)

        @pl.loop(0, count)
        def _(i):
            block = block_in(z, i)
            pick, weight = pick_of(block)
            turned = jnp.where(pick, 1.0, 0.0).T.astype(BF16)
            at = pl.ds(pl.multiple_of(i * slots, slots), slots)
            parts[lax.div(i, ny), lax.rem(i, ny)] = dot(turned, scaled[at]).astype(BF16)
            value = jnp.sum(jnp.where(pick, slot_w[1, at, 0:1], 0.0), axis=0, keepdims=True)
            gate_send[block] = jnp.broadcast_to(value, (8, tokens))

    step = 16

    def by_rows(act):
        @pl.loop(0, tokens // step)
        def _(r):
            act(pl.ds(pl.multiple_of(r * step, step), step))

    def core_copy(j):
        slot = lax.rem(j, 2)
        return remote(parts.at[1 - core], core_recv.at[slot], c_send_sem.at[slot], c_recv_sem.at[slot], sibling)

    def y_copy(j, i):
        return remote(
            y_send.at[j, y_peer(i)], y_recv.at[j, ny - 1 - i],
            y_send_sem.at[j, i - 1], y_recv_sem.at[j, ny - 1 - i], number(zz, y_peer(i), core),
        )

    def core_finish(j):
        core_copy(j).wait()
        slot = lax.rem(j, 2)
        for y in range(ny):

            def act(at):
                both = parts[core, y, at].astype(F32) + core_recv[slot, y, at].astype(F32)
                y_send[j, y, at] = both.astype(BF16)

            by_rows(act)
        for i in range(1, ny):
            y_copy(j, i).start()

    def z_copy(z):
        return remote(
            z_send.at[z], z_recv.at[zz], z_send_sem.at[z], z_recv_sem.at[zz], number(z, yy, core)
        )

    def z_from(z):
        return remote(z_send.at[z], z_recv.at[z], z_send_sem.at[z], z_recv_sem.at[z], number(z, yy, core))

    def y_finish(j):
        z = column_of(j)
        for i in range(1, ny):
            y_copy(j, i).wait_recv()

        def summed(at):
            value = y_send[j, yy, at].astype(F32)
            for i in range(ny - 1):
                value = value + y_recv[j, i, at].astype(F32)
            return value

        @pl.when(z == zz)
        def _():
            def act(at):
                total[at] = summed(at)

            by_rows(act)

        @pl.when(z != zz)
        def _():
            def act(at):
                z_send[z, at] = summed(at).astype(BF16)

            by_rows(act)
            z_copy(z).start()

    @pl.loop(0, nz)
    def _(j):
        far = j + 1

        @pl.when(zz - far >= 0)
        def _():
            arrived(number(zz - far, yy, core))
            plane_sends(zz - far, lambda c: c.start())

        @pl.when(zz + far < nz)
        def _():
            arrived(number(zz + far, yy, core))
            plane_sends(zz + far, lambda c: c.start())

        z = column_of(j)
        for i in range(1, ny):
            block = number(z, y_peer(i), core)
            arrived(block)
            spread(block, 0, sibling).start()
        for y in range(ny):
            arrived(number(z, y, 1 - core))
        compute(z)
        core_copy(j).start()

        @pl.when(j > 0)
        def _():
            y_finish(j - 1)

        core_finish(j)

    def g_copy(target):
        return remote(gate_send.at[target], gates_ref.at[me], g_send.at[target], g_recv.at[me], target)

    def g_from(source):
        return remote(gate_send.at[source], gates_ref.at[source], g_send.at[source], g_recv.at[source], source)

    @pl.loop(1, peers)
    def _(i):
        g_copy(lax.rem(me + i, peers)).start()

    gates_ref[me] = gate_send[me]
    own_grad = pltpu.make_async_copy(grad_ref, blocks.at[0, 0], own_sem.at[0])
    own_grad.start()

    @pl.when(stage == pipes - 1)
    def _():
        zeros[...] = jnp.zeros_like(zeros)
        pltpu.make_async_copy(zeros, out_ref, zero_sem).start()

    y_finish(nz - 1)
    own_grad.wait()

    @pl.loop(0, nz)
    def _(z):
        @pl.when(z != zz)
        def _():
            z_from(z).wait_recv()

    z_recv[zz] = jnp.zeros_like(z_recv[0])

    def finish(at):
        value = blocks[0, 0, at].astype(F32) + total[at]
        for z in range(nz):
            value = value + z_recv[z, at].astype(F32)
        final[at] = value.astype(BF16)

    by_rows(finish)

    passing = pltpu.make_async_remote_copy(
        src_ref=final, dst_ref=out_ref, send_sem=p_sem.at[0], recv_sem=p_sem.at[1],
        device_id={"pipe": lax.rem(stage + pipes - 1, pipes)}, device_id_type=MESH,
    )

    @pl.when(stage > 0)
    def _():
        passing.start()

    @pl.loop(1, peers)
    def _(i):
        other = lax.rem(me + i, peers)
        g_from(other).wait_recv()
        g_copy(other).wait_send()
        w_copy(other).wait_send()

    @pl.loop(0, nz)
    def _(z):
        plane_sends(z, lambda c: c.wait_send())
        for i in range(1, ny):
            spread(number(z, y_peer(i), core), 0, sibling).wait_send()
            y_copy(z, i).wait_send()

        @pl.when(z != zz)
        def _():
            z_copy(z).wait_send()

    @pl.when(stage > 0)
    def _():
        passing.wait_send()

    @pl.when(stage < pipes - 1)
    def _():
        passing.wait_recv()

    @pl.when(stage == pipes - 1)
    def _():
        pltpu.make_async_copy(zeros, out_ref, zero_sem).wait()


def body(pipes, out_grad, layer_input, route_ids, route_probs, gate_weight, up_weight, down_weight):
    ids, probs = route_ids[0], route_probs[0]
    peers = lax.axis_size("expert")
    tokens, top = ids.shape
    width, inner = gate_weight.shape[2:]
    cap = min(tokens, 7 * tokens * top // (6 * peers))
    slots = -(-cap // 16) * 16
    chips = peers // 2
    nz = 4 if chips % 4 == 0 else chips
    ny = chips // nz
    count = 2 * ny
    chosen = ids.T[:, None, :] == jnp.arange(peers, dtype=jnp.int32)[None, :, None]
    weights = jnp.sum(jnp.where(chosen, probs.T[:, None, :], 0.0), axis=0)
    weights = jnp.broadcast_to(weights[:, None, :], (peers, 8, tokens))
    anywhere = pl.BlockSpec(memory_space=pl.ANY)
    vmem = pl.BlockSpec(memory_space=pltpu.VMEM)
    dma = pltpu.SemaphoreType.DMA
    half = (tokens, width)
    passed, gates, unused = pl.pallas_call(
        functools.partial(kernel, nz, ny, slots, pipes),
        out_shape=(
            jax.ShapeDtypeStruct(half, BF16),
            jax.ShapeDtypeStruct((peers, 8, tokens), F32),
            jax.ShapeDtypeStruct((peers, 2) + half, BF16),
        ),
        in_specs=[anywhere, anywhere, vmem, anywhere, anywhere, anywhere],
        out_specs=(anywhere, vmem, anywhere),
        scratch_shapes=[
            pltpu.VMEM((width, inner), BF16),
            pltpu.VMEM((width, inner), BF16),
            pltpu.VMEM((inner, width), BF16),
            pltpu.VMEM((count, 2) + half, BF16),
            pltpu.VMEM((2, count * slots, width), BF16),
            pltpu.VMEM((2, ny) + half, BF16),
            pltpu.VMEM((2, count * slots, inner), BF16),
            pltpu.VMEM((count * slots, width), BF16),
            pltpu.VMEM((2, count * slots, 128), F32),
            pltpu.VMEM((peers, 8, tokens), F32),
            pltpu.VMEM((peers, 8, tokens), F32),
            pltpu.VMEM((2, ny) + half, BF16),
            pltpu.VMEM((nz, ny) + half, BF16),
            pltpu.VMEM((nz, ny - 1) + half, BF16),
            pltpu.VMEM((nz,) + half, BF16),
            pltpu.VMEM((nz,) + half, BF16),
            pltpu.VMEM(half, F32),
            pltpu.VMEM(half, BF16),
            pltpu.VMEM(half, BF16),
            dma((3,)), dma((2,)), dma((count,)), dma(()),
            dma((peers, 2 + ny)), dma((peers,)), dma((peers,)), dma((peers,)),
            dma((peers,)), dma((peers,)),
            dma((2,)), dma((2,)), dma((nz, ny - 1)), dma((nz, ny - 1)), dma((nz,)), dma((nz,)), dma((2,)),
        ],
        compiler_params=pltpu.CompilerParams(
            collective_id=0, has_side_effects=True, vmem_limit_bytes=63 * 2**20
        ),
        cost_estimate=pl.CostEstimate(
            flops=10 * peers * cap * width * inner, bytes_accessed=80 * 2**20, transcendentals=0
        ),
    )(out_grad[0], layer_input[0], weights, gate_weight[0, 0], up_weight[0, 0], down_weight[0, 0])
    slot = jnp.sum(jnp.where(chosen, gates[:, 0, :][None], 0.0), axis=1)
    return passed[None], slot.T.astype(BF16)[None]


def solution(mesh):
    rows = P("pipe", "expert", None)
    mats = P("pipe", "expert", None, None)
    return jax.shard_map(
        functools.partial(body, mesh.shape["pipe"]),
        mesh=mesh,
        in_specs=(rows,) * 4 + (mats,) * 3,
        out_specs=(rows, rows),
        check_vma=False,
    )
```

```python
import functools

import jax
import jax.numpy as jnp
from jax import lax
from jax.experimental import pallas as pl
from jax.experimental.pallas import tpu as pltpu
from jax.sharding import PartitionSpec as P

F32, BF16 = jnp.float32, jnp.bfloat16
MESH = pl.DeviceIdType.MESH
NT = (((1,), (1,)), ((), ()))


def dot(a, b, dims=(((1,), (0,)), ((), ()))):
    return lax.dot_general(a, b, dims, preferred_element_type=F32)


def kernel(
    nz, ny, slots, pipes,
    grad_ref, input_ref, send_w_ref, gate_hbm, up_hbm, down_hbm,
    out_ref, gates_ref, all_ref,
    gate_w, up_w, down_w, blocks, rows, parts, hidden, scaled, slot_w, route, gate_send,
    core_recv, y_send, y_recv, z_send, z_recv, grad_recv,
    load_sem, own_sem, block_sem, ag_send, ag_recv, w_send, w_recv, g_send, g_recv,
    c_send_sem, c_recv_sem, y_send_sem, y_recv_sem, z_send_sem, z_recv_sem, p_sem,
):
    peers = nz * ny * 2
    count = 2 * ny
    tokens, width = grad_ref.shape
    inner = gate_w.shape[1]
    stage = lax.axis_index("pipe")
    me = lax.axis_index("expert")
    core = lax.rem(me, 2)
    yy = lax.rem(lax.div(me, 2), ny)
    zz = lax.div(me, 2 * ny)
    sibling = me + 1 - 2 * core

    def number(z, y, c):
        return (z * ny + y) * 2 + c

    def column_of(j):
        low, high = zz, nz - 1 - zz
        near = jnp.minimum(low, high)
        half = lax.div(j + 1, 2)
        between = jnp.where(lax.rem(j, 2) == 1, zz - half, zz + half)
        far = jnp.where(low <= high, j, nz - 1 - j)
        return jnp.where(j <= 2 * near, between, far)

    def remote(src, dst, ssem, rsem, target):
        return pltpu.make_async_remote_copy(
            src_ref=src, dst_ref=dst, send_sem=ssem, recv_sem=rsem,
            device_id={"expert": target}, device_id_type=MESH,
        )

    def spread(block, kind, target):
        return remote(all_ref.at[block], all_ref.at[block], ag_send.at[block, kind], ag_recv.at[block], target)

    def arrived(block):
        spread(block, 0, sibling).wait_recv()

    def y_peer(i):
        return lax.rem(yy + i, ny)

    def line_sends(z, act):
        block = number(z, yy, core)

        @pl.when((z <= zz) & (zz + 1 < nz))
        def _():
            act(spread(block, 1, me + 2 * ny))

        @pl.when((z >= zz) & (zz > 0))
        def _():
            act(spread(block, 2, me - 2 * ny))

    def side_sends(z, act):
        block = number(z, yy, core)
        act(spread(block, 0, sibling))
        for i in range(1, ny):
            act(spread(block, 2 + i, number(zz, y_peer(i), core)))

    loads = [
        pltpu.make_async_copy(gate_hbm, gate_w, load_sem.at[0]),
        pltpu.make_async_copy(up_hbm, up_w, load_sem.at[1]),
        pltpu.make_async_copy(down_hbm, down_w, load_sem.at[2]),
    ]
    own = [
        pltpu.make_async_copy(grad_ref, all_ref.at[me, 0], own_sem.at[0]),
        pltpu.make_async_copy(input_ref, all_ref.at[me, 1], own_sem.at[1]),
    ]
    for copy in own + loads:
        copy.start()

    barrier = pltpu.get_barrier_semaphore()

    @pl.loop(1, peers)
    def _(i):
        pl.semaphore_signal(barrier, inc=1, device_id={"expert": lax.rem(me + i, peers)}, device_id_type=MESH)

    earlier = lax.rem(stage + pipes - 1, pipes)
    later = lax.rem(stage + 1, pipes)

    @pl.loop(0, nz)
    def _(z):
        for other in (earlier, later):
            pl.semaphore_signal(
                barrier, inc=1, device_id={"pipe": other, "expert": number(z, yy, core)}, device_id_type=MESH
            )

    pl.semaphore_wait(barrier, peers - 1 + 2 * nz)

    def w_copy(target):
        return remote(send_w_ref.at[target], route.at[me], w_send.at[target], w_recv.at[me], target)

    def w_from(source):
        return remote(send_w_ref.at[source], route.at[source], w_send.at[source], w_recv.at[source], source)

    @pl.loop(1, peers)
    def _(i):
        w_copy(lax.rem(me + i, peers)).start()

    for copy in own:
        copy.wait()
    line_sends(zz, lambda c: c.start())
    side_sends(zz, lambda c: c.start())
    passing = pltpu.make_async_remote_copy(
        src_ref=grad_ref, dst_ref=grad_recv, send_sem=p_sem.at[0], recv_sem=p_sem.at[1],
        device_id={"pipe": earlier}, device_id_type=MESH,
    )
    passing.start()
    route[me] = send_w_ref[me]

    @pl.loop(1, peers)
    def _(i):
        w_from(lax.rem(me + i, peers)).wait_recv()

    for copy in loads:
        copy.wait()

    row_at = lax.broadcasted_iota(jnp.int32, (tokens, tokens), 0)
    col_at = lax.broadcasted_iota(jnp.int32, (tokens, tokens), 1)
    before = jnp.where(row_at < col_at, 1.0, 0.0).astype(BF16)
    slot_at = lax.broadcasted_iota(jnp.int32, (slots, tokens), 0)

    def pick_of(block):
        weight = route[block]
        used = jnp.where(weight > 0, 1.0, 0.0)
        place = dot(used.astype(BF16), before)[0:1].astype(jnp.int32)
        return (place == slot_at) & (weight[0:1] > 0), weight[0:1]

    def block_in(g, i):
        k = lax.div(i, 2)
        z = jnp.where(k == 0, column_of(g), column_of(jnp.maximum(g - 1, 0)))
        return number(z, lax.rem(yy + k, ny), lax.rem(i, 2))

    def fetch(g, i):
        return pltpu.make_async_copy(all_ref.at[block_in(g, i)], blocks.at[i], block_sem.at[i])

    def compute(g, first, last):
        span = pl.ds(first * slots, (last - first) * slots)

        @pl.loop(first, last)
        def _(i):
            fetch(g, i).start()

        @pl.loop(first, last)
        def _(i):
            fetch(g, i).wait()
            pick, weight = pick_of(block_in(g, i))
            pick16 = jnp.where(pick, 1.0, 0.0).astype(BF16)
            at = pl.ds(pl.multiple_of(i * slots, slots), slots)
            rows[0, at] = dot(pick16, blocks[i, 0]).astype(BF16)
            rows[1, at] = dot(pick16, blocks[i, 1]).astype(BF16)
            per_slot = jnp.sum(jnp.where(pick, weight, 0.0), axis=1, keepdims=True)
            slot_w[0, at] = jnp.broadcast_to(per_slot, (slots, 128))

        slot_w[1] = jnp.zeros_like(slot_w[1])
        tile = 256

        @pl.loop(0, inner // tile)
        def _(f):
            at = pl.ds(pl.multiple_of(f * tile, tile), tile)
            gate_pre = dot(rows[1, span], gate_w[:, at])
            up_pre = dot(rows[1, span], up_w[:, at])
            back = dot(rows[0, span], down_w[at, :], NT)
            sig = jax.nn.sigmoid(gate_pre)
            up_back = back * (gate_pre * sig)
            hidden[0, span, at] = (back * up_pre * sig * (1.0 + gate_pre * (1.0 - sig))).astype(BF16)
            hidden[1, span, at] = up_back.astype(BF16)
            value = jnp.sum(up_back * up_pre, axis=1, keepdims=True)
            slot_w[1, span] = slot_w[1, span] + jnp.broadcast_to(value, (value.shape[0], 128))

        wide = 512

        @pl.loop(0, width // wide)
        def _(d):
            at = pl.ds(pl.multiple_of(d * wide, wide), wide)
            back = dot(hidden[0, span], gate_w[at, :], NT) + dot(hidden[1, span], up_w[at, :], NT)
            back = back.astype(BF16).astype(F32) * slot_w[0, span, 0:1]
            scaled[span, at] = back.astype(BF16)

        @pl.loop(first, last)
        def _(i):
            block = block_in(g, i)
            pick, weight = pick_of(block)
            turned = jnp.where(pick, 1.0, 0.0).T.astype(BF16)
            at = pl.ds(pl.multiple_of(i * slots, slots), slots)
            parts[lax.rem(i, 2), lax.div(i, 2)] = dot(turned, scaled[at]).astype(BF16)
            value = jnp.sum(jnp.where(pick, slot_w[1, at, 0:1], 0.0), axis=0, keepdims=True)
            gate_send[block] = jnp.broadcast_to(value, (8, tokens))

    step = 16

    def by_rows(act):
        @pl.loop(0, tokens // step)
        def _(r):
            act(pl.ds(pl.multiple_of(r * step, step), step))

    def core_copy(g, first, last):
        slot = lax.rem(g, 2)
        entries = pl.ds(first // 2, (last - first) // 2)
        return remote(
            parts.at[1 - core, entries], core_recv.at[slot, entries],
            c_send_sem.at[slot], c_recv_sem.at[slot], sibling,
        )

    def y_copy(j, i):
        return remote(
            y_send.at[j, i], y_recv.at[j, ny - 1 - i],
            y_send_sem.at[j, i - 1], y_recv_sem.at[j, ny - 1 - i], number(zz, y_peer(i), core),
        )

    def core_finish(g, first, last):
        core_copy(g, first, last).wait()
        slot = lax.rem(g, 2)

        def entry(k, j):
            def act(at):
                both = parts[core, k, at].astype(F32) + core_recv[slot, k, at].astype(F32)
                y_send[j, k, at] = both.astype(BF16)

            by_rows(act)

        for k in range(max(1, first // 2), last // 2):
            entry(k, g - 1)
            y_copy(g - 1, k).start()
        if first == 0:
            entry(0, g)

    def z_copy(z):
        return pltpu.make_async_remote_copy(
            src_ref=z_send.at[z], dst_ref=z_recv.at[zz], send_sem=z_send_sem.at[z], recv_sem=z_recv_sem.at[zz],
            device_id={"pipe": earlier, "expert": number(z, yy, core)}, device_id_type=MESH,
        )

    def z_from(z):
        return pltpu.make_async_remote_copy(
            src_ref=z_send.at[z], dst_ref=z_recv.at[z], send_sem=z_send_sem.at[z], recv_sem=z_recv_sem.at[z],
            device_id={"pipe": earlier, "expert": number(z, yy, core)}, device_id_type=MESH,
        )

    def y_finish(j):
        z = column_of(j)
        for i in range(1, ny):
            y_copy(j, i).wait_recv()

        def act(at):
            value = y_send[j, 0, at].astype(F32)
            for i in range(ny - 1):
                value = value + y_recv[j, i, at].astype(F32)
            z_send[z, at] = value.astype(BF16)

        by_rows(act)
        z_copy(z).start()

    arrived(number(zz, yy, 1 - core))
    compute(0, 0, 2)
    core_copy(0, 0, 2).start()
    core_finish(0, 0, 2)

    def others_in(z):
        for i in range(1, ny):
            block = number(z, y_peer(i), core)
            arrived(block)
            spread(block, 0, sibling).start()

    @pl.loop(1, nz)
    def _(g):
        @pl.when(zz - g >= 0)
        def _():
            arrived(number(zz - g, yy, core))
            line_sends(zz - g, lambda c: c.start())

        @pl.when(zz + g < nz)
        def _():
            arrived(number(zz + g, yy, core))
            line_sends(zz + g, lambda c: c.start())

        z = column_of(g)
        side_sends(z, lambda c: c.start())
        others_in(column_of(g - 1))
        arrived(number(z, yy, 1 - core))
        for i in range(1, ny):
            arrived(number(column_of(g - 1), y_peer(i), 1 - core))
        compute(g, 0, count)
        core_copy(g, 0, count).start()

        @pl.when(g > 1)
        def _():
            y_finish(g - 2)

        core_finish(g, 0, count)

    others_in(column_of(nz - 1))
    for i in range(1, ny):
        arrived(number(column_of(nz - 1), y_peer(i), 1 - core))
    compute(nz, 2, count)
    core_copy(nz, 2, count).start()
    core_finish(nz, 2, count)
    y_finish(nz - 2)

    def g_copy(target):
        return remote(gate_send.at[target], gates_ref.at[me], g_send.at[target], g_recv.at[me], target)

    def g_from(source):
        return remote(gate_send.at[source], gates_ref.at[source], g_send.at[source], g_recv.at[source], source)

    @pl.loop(1, peers)
    def _(i):
        g_copy(lax.rem(me + i, peers)).start()

    gates_ref[me] = gate_send[me]
    y_finish(nz - 1)
    passing.wait_recv()

    @pl.loop(0, nz)
    def _(z):
        z_from(z).wait_recv()

    @pl.when(stage == pipes - 1)
    def _():
        out_ref[...] = jnp.zeros_like(out_ref)

    @pl.when(stage < pipes - 1)
    def _():
        def finish(at):
            value = grad_recv[at].astype(F32)
            for z in range(nz):
                value = value + z_recv[z, at].astype(F32)
            out_ref[at] = value.astype(BF16)

        by_rows(finish)

    @pl.loop(1, peers)
    def _(i):
        other = lax.rem(me + i, peers)
        g_from(other).wait_recv()
        g_copy(other).wait_send()
        w_copy(other).wait_send()

    @pl.loop(0, nz)
    def _(z):
        line_sends(z, lambda c: c.wait_send())
        side_sends(z, lambda c: c.wait_send())
        for i in range(1, ny):
            spread(number(z, y_peer(i), core), 0, sibling).wait_send()
            y_copy(z, i).wait_send()
        z_copy(z).wait_send()

    passing.wait_send()


def body(pipes, out_grad, layer_input, route_ids, route_probs, gate_weight, up_weight, down_weight):
    ids, probs = route_ids[0], route_probs[0]
    peers = lax.axis_size("expert")
    tokens, top = ids.shape
    width, inner = gate_weight.shape[2:]
    cap = min(tokens, 7 * tokens * top // (6 * peers))
    slots = -(-cap // 16) * 16
    chips = peers // 2
    nz = 4 if chips % 4 == 0 else chips
    ny = chips // nz
    count = 2 * ny
    chosen = ids.T[:, None, :] == jnp.arange(peers, dtype=jnp.int32)[None, :, None]
    weights = jnp.sum(jnp.where(chosen, probs.T[:, None, :], 0.0), axis=0)
    weights = jnp.broadcast_to(weights[:, None, :], (peers, 8, tokens))
    anywhere = pl.BlockSpec(memory_space=pl.ANY)
    vmem = pl.BlockSpec(memory_space=pltpu.VMEM)
    dma = pltpu.SemaphoreType.DMA
    half = (tokens, width)
    passed, gates, unused = pl.pallas_call(
        functools.partial(kernel, nz, ny, slots, pipes),
        out_shape=(
            jax.ShapeDtypeStruct(half, BF16),
            jax.ShapeDtypeStruct((peers, 8, tokens), F32),
            jax.ShapeDtypeStruct((peers, 2) + half, BF16),
        ),
        in_specs=[anywhere, anywhere, vmem, anywhere, anywhere, anywhere],
        out_specs=(vmem, vmem, anywhere),
        scratch_shapes=[
            pltpu.VMEM((width, inner), BF16),
            pltpu.VMEM((width, inner), BF16),
            pltpu.VMEM((inner, width), BF16),
            pltpu.VMEM((count, 2) + half, BF16),
            pltpu.VMEM((2, count * slots, width), BF16),
            pltpu.VMEM((2, ny) + half, BF16),
            pltpu.VMEM((2, count * slots, inner), BF16),
            pltpu.VMEM((count * slots, width), BF16),
            pltpu.VMEM((2, count * slots, 128), F32),
            pltpu.VMEM((peers, 8, tokens), F32),
            pltpu.VMEM((peers, 8, tokens), F32),
            pltpu.VMEM((2, ny) + half, BF16),
            pltpu.VMEM((nz, ny) + half, BF16),
            pltpu.VMEM((nz, ny - 1) + half, BF16),
            pltpu.VMEM((nz,) + half, BF16),
            pltpu.VMEM((nz,) + half, BF16),
            pltpu.VMEM(half, BF16),
            dma((3,)), dma((2,)), dma((count,)),
            dma((peers, 2 + ny)), dma((peers,)), dma((peers,)), dma((peers,)),
            dma((peers,)), dma((peers,)),
            dma((2,)), dma((2,)), dma((nz, ny - 1)), dma((nz, ny - 1)), dma((nz,)), dma((nz,)), dma((2,)),
        ],
        compiler_params=pltpu.CompilerParams(
            collective_id=0, has_side_effects=True, vmem_limit_bytes=63 * 2**20
        ),
        cost_estimate=pl.CostEstimate(
            flops=10 * peers * cap * width * inner, bytes_accessed=80 * 2**20, transcendentals=0
        ),
    )(out_grad[0], layer_input[0], weights, gate_weight[0, 0], up_weight[0, 0], down_weight[0, 0])
    slot = jnp.sum(jnp.where(chosen, gates[:, 0, :][None], 0.0), axis=1)
    return passed[None], slot.T.astype(BF16)[None]


def solution(mesh):
    rows = P("pipe", "expert", None)
    mats = P("pipe", "expert", None, None)
    return jax.shard_map(
        functools.partial(body, mesh.shape["pipe"]),
        mesh=mesh,
        in_specs=(rows,) * 4 + (mats,) * 3,
        out_specs=(rows, rows),
        check_vma=False,
    )
```

```python
import functools

import jax
import jax.numpy as jnp
from jax import lax
from jax.experimental import pallas as pl
from jax.experimental.pallas import tpu as pltpu
from jax.sharding import PartitionSpec as P

F32, BF16 = jnp.float32, jnp.bfloat16
MESH = pl.DeviceIdType.MESH
NT = (((1,), (1,)), ((), ()))


def dot(a, b, dims=(((1,), (0,)), ((), ()))):
    return lax.dot_general(a, b, dims, preferred_element_type=F32)


def kernel(
    nz, ny, slots, pipes,
    grad_ref, input_ref, send_w_ref, gate_hbm, up_hbm, down_hbm,
    out_ref, gates_ref, all_ref,
    gate_w, up_w, down_w, blocks, rows, parts, hidden, scaled, slot_w, route, gate_send,
    core_recv, y_send, y_recv, z_send, z_recv, grad_recv,
    load_sem, own_sem, block_sem, ag_send, ag_recv, w_send, w_recv, g_send, g_recv,
    c_send_sem, c_recv_sem, y_send_sem, y_recv_sem, z_send_sem, z_recv_sem, p_sem,
):
    peers = nz * ny * 2
    count = 2 * ny
    tokens, width = grad_ref.shape
    inner = gate_w.shape[1]
    stage = lax.axis_index("pipe")
    me = lax.axis_index("expert")
    core = lax.rem(me, 2)
    yy = lax.rem(lax.div(me, 2), ny)
    zz = lax.div(me, 2 * ny)
    sibling = me + 1 - 2 * core

    def number(z, y, c):
        return (z * ny + y) * 2 + c

    def column_of(j):
        low, high = zz, nz - 1 - zz
        near = jnp.minimum(low, high)
        half = lax.div(j + 1, 2)
        between = jnp.where(lax.rem(j, 2) == 1, zz - half, zz + half)
        far = jnp.where(low <= high, j, nz - 1 - j)
        return jnp.where(j <= 2 * near, between, far)

    def remote(src, dst, ssem, rsem, target):
        return pltpu.make_async_remote_copy(
            src_ref=src, dst_ref=dst, send_sem=ssem, recv_sem=rsem,
            device_id={"expert": target}, device_id_type=MESH,
        )

    def spread(block, kind, target):
        return remote(all_ref.at[block], all_ref.at[block], ag_send.at[block, kind], ag_recv.at[block], target)

    def arrived(block):
        spread(block, 0, sibling).wait_recv()

    def y_peer(i):
        return lax.rem(yy + i, ny)

    def line_sends(z, act):
        block = number(z, yy, core)

        @pl.when((z <= zz) & (zz + 1 < nz))
        def _():
            act(spread(block, 1, me + 2 * ny))

        @pl.when((z >= zz) & (zz > 0))
        def _():
            act(spread(block, 2, me - 2 * ny))

    def side_sends(z, act):
        block = number(z, yy, core)
        act(spread(block, 0, sibling))
        for i in range(1, ny):
            act(spread(block, 2 + i, number(zz, y_peer(i), core)))

    loads = [
        pltpu.make_async_copy(gate_hbm, gate_w, load_sem.at[0]),
        pltpu.make_async_copy(up_hbm, up_w, load_sem.at[1]),
        pltpu.make_async_copy(down_hbm, down_w, load_sem.at[2]),
    ]
    own = [
        pltpu.make_async_copy(grad_ref, all_ref.at[me, 0], own_sem.at[0]),
        pltpu.make_async_copy(input_ref, all_ref.at[me, 1], own_sem.at[1]),
    ]
    for copy in own + loads:
        copy.start()

    barrier = pltpu.get_barrier_semaphore()

    @pl.loop(1, peers)
    def _(i):
        pl.semaphore_signal(barrier, inc=1, device_id={"expert": lax.rem(me + i, peers)}, device_id_type=MESH)

    earlier = lax.rem(stage + pipes - 1, pipes)
    later = lax.rem(stage + 1, pipes)

    @pl.loop(0, nz)
    def _(z):
        for other in (earlier, later):
            pl.semaphore_signal(
                barrier, inc=1, device_id={"pipe": other, "expert": number(z, yy, core)}, device_id_type=MESH
            )

    pl.semaphore_wait(barrier, peers - 1 + 2 * nz)

    def w_copy(target):
        return remote(send_w_ref.at[target], route.at[me], w_send.at[target], w_recv.at[me], target)

    def w_from(source):
        return remote(send_w_ref.at[source], route.at[source], w_send.at[source], w_recv.at[source], source)

    @pl.loop(1, peers)
    def _(i):
        w_copy(lax.rem(me + i, peers)).start()

    for copy in own:
        copy.wait()
    line_sends(zz, lambda c: c.start())
    side_sends(zz, lambda c: c.start())
    passing = pltpu.make_async_remote_copy(
        src_ref=grad_ref, dst_ref=grad_recv, send_sem=p_sem.at[0], recv_sem=p_sem.at[1],
        device_id={"pipe": earlier}, device_id_type=MESH,
    )
    passing.start()
    route[me] = send_w_ref[me]

    @pl.loop(1, peers)
    def _(i):
        w_from(lax.rem(me + i, peers)).wait_recv()

    for copy in loads:
        copy.wait()

    row_at = lax.broadcasted_iota(jnp.int32, (tokens, tokens), 0)
    col_at = lax.broadcasted_iota(jnp.int32, (tokens, tokens), 1)
    before = jnp.where(row_at < col_at, 1.0, 0.0).astype(BF16)
    slot_at = lax.broadcasted_iota(jnp.int32, (slots, tokens), 0)

    def pick_of(block):
        weight = route[block]
        used = jnp.where(weight > 0, 1.0, 0.0)
        place = dot(used.astype(BF16), before)[0:1].astype(jnp.int32)
        return (place == slot_at) & (weight[0:1] > 0), weight[0:1]

    def block_in(g, i):
        k = lax.div(i, 2)
        z = jnp.where(k == 0, column_of(g), column_of(jnp.maximum(g - 1, 0)))
        return number(z, lax.rem(yy + k, ny), lax.rem(i, 2))

    def fetch(g, i):
        return pltpu.make_async_copy(all_ref.at[block_in(g, i)], blocks.at[i], block_sem.at[i])

    def compute(g, first, last, between=lambda: None):
        span = pl.ds(first * slots, (last - first) * slots)

        @pl.loop(first, last)
        def _(i):
            fetch(g, i).start()

        @pl.loop(first, last)
        def _(i):
            fetch(g, i).wait()
            pick, weight = pick_of(block_in(g, i))
            pick16 = jnp.where(pick, 1.0, 0.0).astype(BF16)
            at = pl.ds(pl.multiple_of(i * slots, slots), slots)
            rows[0, at] = dot(pick16, blocks[i, 0]).astype(BF16)
            rows[1, at] = dot(pick16, blocks[i, 1]).astype(BF16)
            per_slot = jnp.sum(jnp.where(pick, weight, 0.0), axis=1, keepdims=True)
            slot_w[0, at] = jnp.broadcast_to(per_slot, (slots, 128))

        slot_w[1] = jnp.zeros_like(slot_w[1])
        tile = 256

        @pl.loop(0, inner // tile)
        def _(f):
            at = pl.ds(pl.multiple_of(f * tile, tile), tile)
            gate_pre = dot(rows[1, span], gate_w[:, at])
            up_pre = dot(rows[1, span], up_w[:, at])
            back = dot(rows[0, span], down_w[at, :], NT)
            sig = jax.nn.sigmoid(gate_pre)
            up_back = back * (gate_pre * sig)
            hidden[0, span, at] = (back * up_pre * sig * (1.0 + gate_pre * (1.0 - sig))).astype(BF16)
            hidden[1, span, at] = up_back.astype(BF16)
            value = jnp.sum(up_back * up_pre, axis=1, keepdims=True)
            slot_w[1, span] = slot_w[1, span] + jnp.broadcast_to(value, (value.shape[0], 128))

        between()
        wide = 512

        @pl.loop(0, width // wide)
        def _(d):
            at = pl.ds(pl.multiple_of(d * wide, wide), wide)
            back = dot(hidden[0, span], gate_w[at, :], NT) + dot(hidden[1, span], up_w[at, :], NT)
            back = back.astype(BF16).astype(F32) * slot_w[0, span, 0:1]
            scaled[span, at] = back.astype(BF16)

        @pl.loop(first, last)
        def _(i):
            block = block_in(g, i)
            pick, weight = pick_of(block)
            turned = jnp.where(pick, 1.0, 0.0).T.astype(BF16)
            at = pl.ds(pl.multiple_of(i * slots, slots), slots)
            parts[lax.rem(i, 2), lax.div(i, 2)] = dot(turned, scaled[at]).astype(BF16)
            value = jnp.sum(jnp.where(pick, slot_w[1, at, 0:1], 0.0), axis=0, keepdims=True)
            gate_send[block] = jnp.broadcast_to(value, (8, tokens))

    step = 16

    def by_rows(act):
        @pl.loop(0, tokens // step)
        def _(r):
            act(pl.ds(pl.multiple_of(r * step, step), step))

    def core_copy(g, first, last):
        slot = lax.rem(g, 2)
        entries = pl.ds(first // 2, (last - first) // 2)
        return remote(
            parts.at[1 - core, entries], core_recv.at[slot, entries],
            c_send_sem.at[slot], c_recv_sem.at[slot], sibling,
        )

    def y_copy(j, i):
        return remote(
            y_send.at[j, i], y_recv.at[j, ny - 1 - i],
            y_send_sem.at[j, i - 1], y_recv_sem.at[j, ny - 1 - i], number(zz, y_peer(i), core),
        )

    def core_finish(g, first, last):
        core_copy(g, first, last).wait()
        slot = lax.rem(g, 2)

        def entry(k, j):
            def act(at):
                both = parts[core, k, at].astype(F32) + core_recv[slot, k, at].astype(F32)
                y_send[j, k, at] = both.astype(BF16)

            by_rows(act)

        for k in range(max(1, first // 2), last // 2):
            entry(k, g - 1)
            y_copy(g - 1, k).start()
        if first == 0:
            entry(0, g)

    def z_copy(z):
        return pltpu.make_async_remote_copy(
            src_ref=z_send.at[z], dst_ref=z_recv.at[zz], send_sem=z_send_sem.at[z], recv_sem=z_recv_sem.at[zz],
            device_id={"pipe": earlier, "expert": number(z, yy, core)}, device_id_type=MESH,
        )

    def z_from(z):
        return pltpu.make_async_remote_copy(
            src_ref=z_send.at[z], dst_ref=z_recv.at[z], send_sem=z_send_sem.at[z], recv_sem=z_recv_sem.at[z],
            device_id={"pipe": earlier, "expert": number(z, yy, core)}, device_id_type=MESH,
        )

    def y_finish(j):
        z = column_of(j)
        for i in range(1, ny):
            y_copy(j, i).wait_recv()

        def act(at):
            value = y_send[j, 0, at].astype(F32)
            for i in range(ny - 1):
                value = value + y_recv[j, i, at].astype(F32)
            z_send[z, at] = value.astype(BF16)

        by_rows(act)
        z_copy(z).start()

    arrived(number(zz, yy, 1 - core))
    compute(0, 0, 2)
    core_copy(0, 0, 2).start()
    core_finish(0, 0, 2)

    def others_in(z):
        for i in range(1, ny):
            block = number(z, y_peer(i), core)
            arrived(block)
            spread(block, 0, sibling).start()

    def advance(g):
        @pl.when(zz - g >= 0)
        def _():
            arrived(number(zz - g, yy, core))
            line_sends(zz - g, lambda c: c.start())

        @pl.when(zz + g < nz)
        def _():
            arrived(number(zz + g, yy, core))
            line_sends(zz + g, lambda c: c.start())

        side_sends(column_of(g), lambda c: c.start())

    advance(1)

    @pl.loop(1, nz)
    def _(g):
        def between():
            @pl.when(g + 1 < nz)
            def _():
                advance(g + 1)

        z = column_of(g)
        others_in(column_of(g - 1))
        arrived(number(z, yy, 1 - core))
        for i in range(1, ny):
            arrived(number(column_of(g - 1), y_peer(i), 1 - core))
        compute(g, 0, count, between)
        core_copy(g, 0, count).start()

        @pl.when(g > 1)
        def _():
            y_finish(g - 2)

        core_finish(g, 0, count)

    others_in(column_of(nz - 1))
    for i in range(1, ny):
        arrived(number(column_of(nz - 1), y_peer(i), 1 - core))
    compute(nz, 2, count)
    core_copy(nz, 2, count).start()
    core_finish(nz, 2, count)
    y_finish(nz - 2)

    def g_copy(target):
        return remote(gate_send.at[target], gates_ref.at[me], g_send.at[target], g_recv.at[me], target)

    def g_from(source):
        return remote(gate_send.at[source], gates_ref.at[source], g_send.at[source], g_recv.at[source], source)

    @pl.loop(1, peers)
    def _(i):
        g_copy(lax.rem(me + i, peers)).start()

    gates_ref[me] = gate_send[me]
    y_finish(nz - 1)
    passing.wait_recv()

    @pl.loop(0, nz)
    def _(z):
        z_from(z).wait_recv()

    @pl.when(stage == pipes - 1)
    def _():
        out_ref[...] = jnp.zeros_like(out_ref)

    @pl.when(stage < pipes - 1)
    def _():
        def finish(at):
            value = grad_recv[at].astype(F32)
            for z in range(nz):
                value = value + z_recv[z, at].astype(F32)
            out_ref[at] = value.astype(BF16)

        by_rows(finish)

    @pl.loop(1, peers)
    def _(i):
        other = lax.rem(me + i, peers)
        g_from(other).wait_recv()
        g_copy(other).wait_send()
        w_copy(other).wait_send()

    @pl.loop(0, nz)
    def _(z):
        line_sends(z, lambda c: c.wait_send())
        side_sends(z, lambda c: c.wait_send())
        for i in range(1, ny):
            spread(number(z, y_peer(i), core), 0, sibling).wait_send()
            y_copy(z, i).wait_send()
        z_copy(z).wait_send()

    passing.wait_send()


def body(pipes, out_grad, layer_input, route_ids, route_probs, gate_weight, up_weight, down_weight):
    ids, probs = route_ids[0], route_probs[0]
    peers = lax.axis_size("expert")
    tokens, top = ids.shape
    width, inner = gate_weight.shape[2:]
    cap = min(tokens, 7 * tokens * top // (6 * peers))
    slots = -(-cap // 16) * 16
    chips = peers // 2
    nz = 4 if chips % 4 == 0 else chips
    ny = chips // nz
    count = 2 * ny
    chosen = ids.T[:, None, :] == jnp.arange(peers, dtype=jnp.int32)[None, :, None]
    weights = jnp.sum(jnp.where(chosen, probs.T[:, None, :], 0.0), axis=0)
    weights = jnp.broadcast_to(weights[:, None, :], (peers, 8, tokens))
    anywhere = pl.BlockSpec(memory_space=pl.ANY)
    vmem = pl.BlockSpec(memory_space=pltpu.VMEM)
    dma = pltpu.SemaphoreType.DMA
    half = (tokens, width)
    passed, gates, unused = pl.pallas_call(
        functools.partial(kernel, nz, ny, slots, pipes),
        out_shape=(
            jax.ShapeDtypeStruct(half, BF16),
            jax.ShapeDtypeStruct((peers, 8, tokens), F32),
            jax.ShapeDtypeStruct((peers, 2) + half, BF16),
        ),
        in_specs=[anywhere, anywhere, vmem, anywhere, anywhere, anywhere],
        out_specs=(vmem, vmem, anywhere),
        scratch_shapes=[
            pltpu.VMEM((width, inner), BF16),
            pltpu.VMEM((width, inner), BF16),
            pltpu.VMEM((inner, width), BF16),
            pltpu.VMEM((count, 2) + half, BF16),
            pltpu.VMEM((2, count * slots, width), BF16),
            pltpu.VMEM((2, ny) + half, BF16),
            pltpu.VMEM((2, count * slots, inner), BF16),
            pltpu.VMEM((count * slots, width), BF16),
            pltpu.VMEM((2, count * slots, 128), F32),
            pltpu.VMEM((peers, 8, tokens), F32),
            pltpu.VMEM((peers, 8, tokens), F32),
            pltpu.VMEM((2, ny) + half, BF16),
            pltpu.VMEM((nz, ny) + half, BF16),
            pltpu.VMEM((nz, ny - 1) + half, BF16),
            pltpu.VMEM((nz,) + half, BF16),
            pltpu.VMEM((nz,) + half, BF16),
            pltpu.VMEM(half, BF16),
            dma((3,)), dma((2,)), dma((count,)),
            dma((peers, 2 + ny)), dma((peers,)), dma((peers,)), dma((peers,)),
            dma((peers,)), dma((peers,)),
            dma((2,)), dma((2,)), dma((nz, ny - 1)), dma((nz, ny - 1)), dma((nz,)), dma((nz,)), dma((2,)),
        ],
        compiler_params=pltpu.CompilerParams(
            collective_id=0, has_side_effects=True, vmem_limit_bytes=63 * 2**20
        ),
        cost_estimate=pl.CostEstimate(
            flops=10 * peers * cap * width * inner, bytes_accessed=80 * 2**20, transcendentals=0
        ),
    )(out_grad[0], layer_input[0], weights, gate_weight[0, 0], up_weight[0, 0], down_weight[0, 0])
    slot = jnp.sum(jnp.where(chosen, gates[:, 0, :][None], 0.0), axis=1)
    return passed[None], slot.T.astype(BF16)[None]


def solution(mesh):
    rows = P("pipe", "expert", None)
    mats = P("pipe", "expert", None, None)
    return jax.shard_map(
        functools.partial(body, mesh.shape["pipe"]),
        mesh=mesh,
        in_specs=(rows,) * 4 + (mats,) * 3,
        out_specs=(rows, rows),
        check_vma=False,
    )
```
